128 devices in a mesh: cells: 16 (over x, z_lo, core), pairs: 8 (over y, z_hi).
Axes of the slice: x: 4, y: 4, z: 4 (z_hi: 2, z_lo: 2; z = z_hi * 2 + z_lo), core: 2. Of those that a mesh axis runs over, the one named last changes fastest.
Arguments:
- number: float32 [64, 128, 4096], P(None, None, 'cells'), may hold values from 0.25 to 2.5
- mix: float32 [3, 4096], P(None, 'cells'), may hold values from 0.05 to 0.3
- neighbours: int32 [3, 4096], P(None, 'cells'), may hold values from 0 to 383, as said below
- sends: int32 [2, 1024], P(None, 'cells'), may hold values from 0 to 255, as said below
- kernel: float32 [128, 128], replicated, may hold values from 0.0005 to 0.005
- growth: float32 [128], replicated, may hold values from 0.05 to 0.5
- brk_rate: float32 [128], replicated, may hold values from 0.02 to 0.3
- brk_target: int32 [2, 128], replicated, may hold values from 0 to 126, as said below
Outputs:
- updated: float32 [64, 128, 4096], P(None, 'pairs', 'cells')
The draws below stay inside these ranges and needn't reach their ends.
Inputs may be any that keep to these rules, and one draw needn't show every extreme that they name: `sends`: within one partition's block of 64 entries of a row the columns are distinct, each in 0 to 255. `neighbours`: partition 0 never names the lower partition's slots and the last partition never names the upper partition's; every other partition names each of its 128 received slots. `brk_target`: each target of pivot i is below i; both targets of pivot 0 are 0.
All inputs are finite; a program needn't handle non-finite values.
Results may differ from the reference program's by a relative error of at most 0.00005.
Values sent between devices are 32-bit elements; how exact they have to be, the bound alone decides.
No kernel may reach another device: no remote copies, remote signals or barrier semaphores. Data moves between devices by JAX's collectives and lax.ppermute only.
A program may use at most 128 MiB of HBM per device.

```python
import math
import jax
import jax.numpy as jnp
from jax import lax

P_SIZE = 128
LEV = 64
COLS_DEV = 256
HALO = 64
NCOLS = 4096
N_CELLS = 16


def draw_sends(key, part):
    scores = jax.random.randint(key, (2, N_CELLS, COLS_DEV), 0, 1 << 20) * COLS_DEV + jnp.arange(COLS_DEV, dtype=jnp.int32)
    order = jnp.argsort(scores, axis=2)[:, :, :HALO]
    return order.reshape(2, N_CELLS * HALO).astype(jnp.int32)


def draw_neighbours(key, part):
    column = jnp.arange(NCOLS, dtype=jnp.int32)
    device = column // COLS_DEV
    local_col = column % COLS_DEV
    key_a, key_b, key_c = jax.random.split(key, 3)

    def nearby(sub):
        return (local_col + jax.random.randint(sub, (NCOLS,), 1, COLS_DEV)) % COLS_DEV
    row_a = nearby(key_a)
    row_b = jnp.where((local_col < HALO) & (device > 0), COLS_DEV + local_col, nearby(key_b))
    row_c = jnp.where((local_col >= COLS_DEV - HALO) & (device < N_CELLS - 1), COLS_DEV + HALO + local_col - (COLS_DEV - HALO), nearby(key_c))
    return jnp.stack([row_a, row_b, row_c]).astype(jnp.int32)


def draw_brk_target(key, part):
    index = jnp.arange(P_SIZE, dtype=jnp.int32)
    nearest = jnp.maximum(index - 1, 0)
    farther = jax.random.randint(key, (P_SIZE,), 0, jnp.maximum(index, 1))
    return jnp.stack([nearest, farther]).astype(jnp.int32)


def block_scale(rng, dims, cuts, smallest, top_value):
    factor_of = 1.0
    for position, parts in cuts:
        draws = jax.random.uniform(jax.random.fold_in(jax.random.fold_in(rng, 6), position), (parts,), jnp.float32, smallest / len(cuts), top_value / len(cuts))
        factor_of = factor_of * jnp.repeat(jnp.exp(draws), dims[position] // parts).reshape((-1,) + (1,) * (len(dims) - 1 - position))
    return factor_of


def setup_inputs(seed: int = 0) -> dict:
    arg_keys = jax.random.split(jax.random.key(seed), 9)
    number = jnp.clip(jnp.exp(math.log(2.5) - 2.3025851 * jax.random.uniform(arg_keys[0], (LEV, P_SIZE, NCOLS), jnp.float32) ** block_scale(arg_keys[0], (LEV, P_SIZE, NCOLS), ((2, 16),), -0.2, 0.2)), 0.25, 2.5)
    mix = jnp.clip(0.05 + 0.25 * jax.random.uniform(arg_keys[1], (3, NCOLS), jnp.float32) ** block_scale(arg_keys[1], (3, NCOLS), ((1, 16),), -0.2, 0.2), 0.05, 0.3)
    neighbours = draw_neighbours(jax.random.fold_in(arg_keys[8], 71), 0)
    sends = draw_sends(jax.random.fold_in(arg_keys[8], 71), 0)
    kernel = jnp.clip(jnp.exp(jax.random.uniform(arg_keys[4], (P_SIZE, P_SIZE), jnp.float32, math.log(0.0005), math.log(0.005))), 0.0005, 0.005)
    growth = jnp.clip(jnp.exp(jax.random.uniform(arg_keys[5], (P_SIZE,), jnp.float32, math.log(0.05), math.log(0.5))), 0.05, 0.5)
    brk_rate = jnp.clip(jnp.exp(jax.random.uniform(arg_keys[6], (P_SIZE,), jnp.float32, math.log(0.02), math.log(0.3))), 0.02, 0.3)
    brk_target = draw_brk_target(jax.random.fold_in(arg_keys[8], 71), 0)
    return dict(number=number, mix=mix, neighbours=neighbours, sends=sends, kernel=kernel, growth=growth, brk_rate=brk_rate, brk_target=brk_target)


def share_of(target, volume, count):
    vk = jnp.exp2(target * 0.25)
    vprev = jnp.exp2((target - 1.0) * 0.25)
    vnext = jnp.exp2((target + 1.0) * 0.25)
    lower = jnp.where((target >= 1.0) & (volume > vprev) & (volume <= vk), (volume - vprev) / (vk - vprev), 0.0)
    upper = jnp.where((target <= count - 2.0) & (volume > vk) & (volume < vnext), (vnext - volume) / (vnext - vk), 0.0)
    top = jnp.where((target == count - 1.0) & (volume > vk), volume / vk, 0.0)
    return lower + upper + top


def reference(number, mix, neighbours, sends, kernel, growth, brk_rate, brk_target):
    levels, piv, ncols = number.shape
    cols = COLS_DEV
    halo_w = HALO
    column = jnp.arange(ncols, dtype=jnp.int32)
    device = column // cols
    moved = number
    for edge in range(3):
        slot = neighbours[edge]
        below = device - 1
        above = device + 1
        low_pos = jnp.clip(below * halo_w + slot - cols, 0, N_CELLS * halo_w - 1)
        high_pos = jnp.clip(above * halo_w + slot - cols - halo_w, 0, N_CELLS * halo_w - 1)
        src_low = below * cols + sends[0][low_pos]
        src_high = above * cols + sends[1][high_pos]
        source = jnp.where(slot < cols, device * cols + slot, jnp.where(slot < cols + halo_w, src_low, src_high))
        valid = jnp.where(slot < cols, True, jnp.where(slot < cols + halo_w, below >= 0, above < N_CELLS))
        source = jnp.clip(source, 0, ncols - 1).astype(jnp.int32)
        value = jnp.where(valid[None, None, :], jnp.take(number, source, axis=2), jnp.float32(0.0))
        moved = moved + mix[edge][None, None, :] * (value - number)
    sym = 0.5 * (kernel + kernel.T)
    index = jnp.arange(piv, dtype=jnp.int32)
    first = index[:, None]
    second = index[None, :]
    mask = jnp.where(second < first, 1.0, jnp.where(second == first, 0.5, 0.0)).astype(jnp.float32)
    weight = (sym * mask).reshape(-1)
    volume = (jnp.exp2(first.astype(jnp.float32) * 0.25) + jnp.exp2(second.astype(jnp.float32) * 0.25)).reshape(-1)
    pivots = jnp.exp2(index.astype(jnp.float32) * 0.25)
    k_low = (jnp.sum((pivots[None, :] <= volume[:, None]).astype(jnp.int32), axis=1) - 1).astype(jnp.int32)
    k_high = jnp.minimum(k_low + 1, piv - 1).astype(jnp.int32)
    eta_low = share_of(k_low.astype(jnp.float32), volume, float(piv))
    eta_high = jnp.where(k_low < piv - 1, share_of(k_high.astype(jnp.float32), volume, float(piv)), 0.0)

    def level_birth(field):
        rate = (weight.reshape(piv, piv)[:, :, None] * field[:, None, :] * field[None, :, :]).reshape(piv * piv, ncols)
        part_low = jax.ops.segment_sum(eta_low[:, None] * rate, k_low, num_segments=piv)
        part_high = jax.ops.segment_sum(eta_high[:, None] * rate, k_high, num_segments=piv)
        return part_low + part_high

    birth = lax.map(level_birth, moved)
    loss = moved * jnp.einsum("ij,ljc->lic", sym, moved, precision=lax.Precision.HIGHEST)
    flux = growth[None, :, None] * moved
    inflow = jnp.concatenate([jnp.zeros_like(flux[:, :1]), flux[:, :-1]], axis=1)
    grow = inflow - flux
    counts = (brk_target[0][None, :] == index[:, None]).astype(jnp.float32) + (brk_target[1][None, :] == index[:, None]).astype(jnp.float32)
    matrix = counts * brk_rate[None, :] - jnp.where(first == second, brk_rate[None, :], 0.0)
    gain = jnp.einsum("ki,lic->lkc", matrix, moved, precision=lax.Precision.HIGHEST)
    return moved + birth - loss + grow + gain
```

```python
import functools

import jax
import jax.numpy as jnp
import numpy as np
from jax import lax
from jax.experimental import pallas as pl
from jax.experimental.pallas import tpu as pltpu
from jax.sharding import PartitionSpec as P

PIV = 128
COLS = 256
SLOTS = 64
OWN = 16
WIN = 32
ROWS = WIN + 3 * OWN
STEP = 8
F32 = jnp.float32
BF16 = jnp.bfloat16


def share_tables():
    v = 2.0 ** (np.arange(PIV) / 4.0)
    tables = np.zeros((5, PIV, PIV))
    for m in range(5):
        for k in range(m, PIV):
            i = k - m
            for j in range(i + 1):
                u = 2.0 ** ((i + 4) / 4.0) if i == j else v[i] + v[j]
                if i == j and i + 4 < PIV:
                    u = v[i + 4]
                share = 0.0
                if k >= 1 and v[k - 1] < u <= v[k]:
                    share = (u - v[k - 1]) / (v[k] - v[k - 1])
                elif k <= PIV - 2 and v[k] < u < v[k + 1]:
                    share = (v[k + 1] - u) / (v[k + 1] - v[k])
                elif k == PIV - 1 and u > v[k]:
                    share = u / v[k]
                tables[m, k, j] = share * (0.5 if i == j else 1.0)
    return tables.astype(np.float32)


def split(x):
    hi = x.astype(BF16)
    return hi, (x - hi.astype(F32)).astype(BF16)


def dot(a, b):
    return jnp.dot(a, b, preferred_element_type=F32)


def iota(shape, axis):
    return lax.broadcasted_iota(jnp.int32, shape, axis)


def symmetric(kernel_ref):
    k = kernel_ref[...]
    return 0.5 * (k + k.T)


def fill_functionals(full, kernel_ref, growth_ref, rate_ref, target_ref, table_ref):
    sym = symmetric(kernel_ref)
    full[0] = sym * (table_ref[0] - 1.0)
    full[1] = pltpu.roll(sym, 1, 0) * table_ref[1]
    row, col = iota((PIV, PIV), 0), iota((PIV, PIV), 1)
    rate, growth = rate_ref[...], growth_ref[...]
    counts = (target_ref[0:1, :] == row).astype(F32) + (target_ref[1:2, :] == row).astype(F32)
    full[2] = (
        counts * rate
        + jnp.where(row == col, 1.0 - growth - rate, 0.0)
        + jnp.where(row == col + 1, growth, 0.0)
    )


def functionals(full, rank):
    start = pl.multiple_of(rank * OWN, OWN)
    window = iota((WIN, PIV), 1) == iota((WIN, PIV), 0) + (start - (WIN - OWN))
    rows = jnp.concatenate(
        [window.astype(F32)] + [full[m, pl.ds(start, OWN), :] for m in range(3)], axis=0
    )
    hi, lo = split(rows)
    return jnp.concatenate([hi, hi, lo], axis=1)


def ranks():
    rank = lax.axis_index("pairs")
    part = lax.rem(lax.axis_index("cells"), 4)
    flip = lax.rem(rank, 2) * -2 + 1
    to_up = rank + jnp.where(part == 3, flip, 0)
    to_down = rank + jnp.where(part == 0, flip, 0)
    return rank, to_up, to_down


def halo_kernel(
    number, sends, kernel, growth, rate, target, table, up, down, full, pick, func
):
    @pl.when(pl.program_id(0) == 0)
    def _():
        _, to_up, to_down = ranks()
        fill_functionals(full, kernel, growth, rate, target, table)
        func[0] = functionals(full, to_up)
        func[1] = functionals(full, to_down)
        a, b = sends[0:1, :], sends[1:2, :]
        named = jnp.concatenate([a, a + COLS, b, b + COLS], axis=1)
        pick[...] = (iota((2 * COLS, 4 * SLOTS), 0) == named).astype(BF16)

    pairs = STEP // 2
    both = jnp.concatenate(
        [jnp.concatenate([number[2 * q], number[2 * q + 1]], axis=1) for q in range(pairs)],
        axis=0,
    )
    hi, lo = split(both)
    got_hi = dot(hi, pick[...]).astype(BF16)
    got_lo = dot(lo, pick[...]).astype(BF16)
    for q in range(pairs):
        rows = slice(q * PIV, (q + 1) * PIV)
        for way, out in ((0, up), (1, down)):
            lanes = slice(way * 2 * SLOTS, (way + 1) * 2 * SLOTS)
            h, l = got_hi[rows, lanes], got_lo[rows, lanes]
            out[q] = dot(func[way], jnp.concatenate([h, l, h], axis=0))


def local_kernel(
    number, mix, neighbours, kernel, growth, rate, target, table, base, full, mixing, func
):
    @pl.when(pl.program_id(0) == 0)
    def _():
        rank, _, _ = ranks()
        fill_functionals(full, kernel, growth, rate, target, table)
        func[...] = functionals(full, rank)
        row, col = iota((COLS, COLS), 0), iota((COLS, COLS), 1)
        m = mix[...]
        total = jnp.where(row == col, 1.0 - m[0:1] - m[1:2] - m[2:3], 0.0)
        for e in range(3):
            total = total + jnp.where(neighbours[e : e + 1, :] == row, m[e : e + 1], 0.0)
        mixing[0], mixing[1] = split(total)

    parts = []
    for l in range(STEP):
        h, lo = split(number[l])
        parts.append(dot(func[...], jnp.concatenate([h, lo, h], axis=0)))
    t_hi, t_lo = split(jnp.concatenate(parts, axis=0))
    mixed = dot(t_hi, mixing[0]) + dot(t_lo, mixing[0]) + dot(t_hi, mixing[1])
    base[...] = mixed.reshape(STEP, ROWS, COLS)


def update_kernel(base, low, high, mix, neighbours, kernel, table, out, mixing, band):
    @pl.when(pl.program_id(0) == 0)
    def _():
        rank, _, _ = ranks()
        row = iota((4 * SLOTS, COLS), 0)
        inner = lax.rem(row, 2 * SLOTS)
        for a in range(2):
            slot = COLS + jnp.where(row < 2 * SLOTS, 0, SLOTS) + inner - a * SLOTS
            slot = jnp.where((inner >= a * SLOTS) & (inner < (a + 1) * SLOTS), slot, -1)
            total = jnp.zeros((4 * SLOTS, COLS), F32)
            for e in range(3):
                total = total + jnp.where(
                    neighbours[e : e + 1, :] == slot, mix[e : e + 1, :], 0.0
                )
            hi, lo = split(total)
            mixing[0, :, a * COLS : (a + 1) * COLS] = hi
            mixing[1, :, a * COLS : (a + 1) * COLS] = lo
        sym = symmetric(kernel)
        start = pl.multiple_of(rank * OWN, OWN)
        shift = lax.rem(PIV + (WIN - OWN) - rank * OWN, PIV)
        rows = []
        for m in range(2, 5):
            band[0] = pltpu.roll(sym, m, 0) * table[m]
            rows.append(band[0, pl.ds(start, OWN), :])
        moved = pltpu.roll(jnp.concatenate(rows, axis=0), shift, 1)
        band[1, 0 : 3 * OWN, :] = moved

    pairs = STEP // 2
    both = jnp.concatenate(
        [jnp.concatenate([low[q], high[q]], axis=1) for q in range(pairs)], axis=0
    )
    hi, lo = split(both)
    came = dot(hi, mixing[0]) + dot(lo, mixing[0]) + dot(hi, mixing[1])
    w_hi, w_lo = split(band[1, 0 : 3 * OWN, 0:WIN])
    weights = jnp.concatenate([w_hi, w_hi, w_lo], axis=1)
    for l in range(STEP):
        q, a = l // 2, l % 2
        v = base[l] + came[q * ROWS : (q + 1) * ROWS, a * COLS : (a + 1) * COLS]
        window = v[0:WIN]
        n_hi, n_lo = split(window)
        births = dot(weights, jnp.concatenate([n_hi, n_lo, n_hi], axis=0))
        own = WIN - OWN
        total = v[WIN + 2 * OWN : WIN + 3 * OWN] + window[own:] * v[WIN : WIN + OWN]
        total = total + window[own - 1 : WIN - 1] * v[WIN + OWN : WIN + 2 * OWN]
        for m in range(2, 5):
            total = total + window[own - m : WIN - m] * births[(m - 2) * OWN : (m - 1) * OWN]
        out[l] = total


def whole(shape):
    return pl.BlockSpec(shape, lambda s: (0,) * len(shape))


def on_device(number, mix, neighbours, sends, kernel, growth, brk_rate, brk_target):
    levels = number.shape[0]
    steps = levels // STEP
    growth = growth.reshape(1, PIV)
    rate = brk_rate.reshape(1, PIV)
    table = jnp.asarray(share_tables())
    number_spec = pl.BlockSpec((STEP, PIV, COLS), lambda s: (s, 0, 0))
    half_spec = pl.BlockSpec((STEP // 2, ROWS, 2 * SLOTS), lambda s: (s, 0, 0))
    base_spec = pl.BlockSpec((STEP, ROWS, COLS), lambda s: (s, 0, 0))
    weights = [whole((PIV, PIV)), whole((1, PIV)), whole((1, PIV)), whole((2, PIV)), whole((5, PIV, PIV))]
    half = jax.ShapeDtypeStruct((levels // 2, ROWS, 2 * SLOTS), F32)
    params = pltpu.CompilerParams(vmem_limit_bytes=40 * 2**20)

    up, down = pl.pallas_call(
        halo_kernel,
        grid=(steps,),
        in_specs=[number_spec, whole((2, SLOTS))] + weights,
        out_specs=[half_spec, half_spec],
        out_shape=[half, half],
        scratch_shapes=[
            pltpu.VMEM((3, PIV, PIV), F32),
            pltpu.VMEM((2 * COLS, 4 * SLOTS), BF16),
            pltpu.VMEM((2, ROWS, 3 * PIV), BF16),
        ],
        compiler_params=params,
        cost_estimate=pl.CostEstimate(flops=4 * 10**9, bytes_accessed=12 * 10**6, transcendentals=0),
        name="halo",
    )(number, sends, kernel, growth, rate, brk_target, table)

    n_cells, n_pairs = lax.axis_size("cells"), lax.axis_size("pairs")
    up_pairs, down_pairs = [], []
    for d in range(n_cells):
        for p in range(n_pairs):
            if d + 1 < n_cells:
                up_pairs.append((d * n_pairs + p, (d + 1) * n_pairs + (p ^ (d % 4 == 3))))
            if d > 0:
                down_pairs.append((d * n_pairs + p, (d - 1) * n_pairs + (p ^ (d % 4 == 0))))
    low = lax.ppermute(up, ("cells", "pairs"), up_pairs)
    high = lax.ppermute(down, ("cells", "pairs"), down_pairs)

    base = pl.pallas_call(
        local_kernel,
        grid=(steps,),
        in_specs=[number_spec, whole((3, COLS)), whole((3, COLS))] + weights,
        out_specs=base_spec,
        out_shape=jax.ShapeDtypeStruct((levels, ROWS, COLS), F32),
        scratch_shapes=[
            pltpu.VMEM((3, PIV, PIV), F32),
            pltpu.VMEM((2, COLS, COLS), BF16),
            pltpu.VMEM((ROWS, 3 * PIV), BF16),
        ],
        compiler_params=params,
        cost_estimate=pl.CostEstimate(flops=4 * 10**9, bytes_accessed=14 * 10**6, transcendentals=0),
        name="local",
    )(number, mix, neighbours, kernel, growth, rate, brk_target, table)

    return pl.pallas_call(
        update_kernel,
        grid=(steps,),
        in_specs=[
            base_spec,
            half_spec,
            half_spec,
            whole((3, COLS)),
            whole((3, COLS)),
            whole((PIV, PIV)),
            whole((5, PIV, PIV)),
        ],
        out_specs=pl.BlockSpec((STEP, OWN, COLS), lambda s: (s, 0, 0)),
        out_shape=jax.ShapeDtypeStruct((levels, OWN, COLS), F32),
        scratch_shapes=[
            pltpu.VMEM((2, 4 * SLOTS, 2 * COLS), BF16),
            pltpu.VMEM((2, PIV, PIV), F32),
        ],
        compiler_params=params,
        cost_estimate=pl.CostEstimate(flops=3 * 10**9, bytes_accessed=10 * 10**6, transcendentals=0),
        name="update",
    )(base, low, high, mix, neighbours, kernel, table)


def solution(mesh):
    placed = (
        P(None, None, "cells"),
        P(None, "cells"),
        P(None, "cells"),
        P(None, "cells"),
        P(),
        P(),
        P(),
        P(),
    )
    return jax.shard_map(
        on_device, mesh=mesh, in_specs=placed, out_specs=P(None, "pairs", "cells"), check_vma=False
    )
```

```python
import functools

import jax
import jax.numpy as jnp
import numpy as np
from jax import lax
from jax.experimental import pallas as pl
from jax.experimental.pallas import tpu as pltpu
from jax.sharding import PartitionSpec as P

PIV = 128
COLS = 256
SLOTS = 64
OWN = 16
WIN = 32
ROWS = WIN + 3 * OWN
STEP = 8
SPLITS = ()
NEAR = 1
LOAD = 8
AHEAD = 3
LIMITS = (54, 46, 32)
F32 = jnp.float32
BF16 = jnp.bfloat16


def share_tables():
    v = 2.0 ** (np.arange(PIV) / 4.0)
    tables = np.zeros((5, PIV, PIV))
    for m in range(5):
        for k in range(m, PIV):
            i = k - m
            for j in range(i + 1):
                u = 2.0 ** ((i + 4) / 4.0) if i == j else v[i] + v[j]
                if i == j and i + 4 < PIV:
                    u = v[i + 4]
                share = 0.0
                if k >= 1 and v[k - 1] < u <= v[k]:
                    share = (u - v[k - 1]) / (v[k] - v[k - 1])
                elif k <= PIV - 2 and v[k] < u < v[k + 1]:
                    share = (v[k + 1] - u) / (v[k + 1] - v[k])
                elif k == PIV - 1 and u > v[k]:
                    share = u / v[k]
                tables[m, k, j] = share * (0.5 if i == j else 1.0)
    return tables.astype(np.float32)


def split(x):
    hi = x.astype(BF16)
    return hi, (x - hi.astype(F32)).astype(BF16)


def dot(a, b):
    return jnp.dot(a, b, preferred_element_type=F32)


def iota(shape, axis):
    return lax.broadcasted_iota(jnp.int32, shape, axis)


def symmetric(kernel_ref):
    k = kernel_ref[...]
    return 0.5 * (k + k.T)


def fill_functionals(full, kernel_ref, growth_ref, rate_ref, target_ref, table_ref):
    sym = symmetric(kernel_ref)
    full[0] = sym * (table_ref[0] - 1.0)
    full[1] = pltpu.roll(sym, 1, 0) * table_ref[1]
    row, col = iota((PIV, PIV), 0), iota((PIV, PIV), 1)
    rate, growth = rate_ref[...], growth_ref[...]
    counts = (target_ref[0:1, :] == row).astype(F32) + (target_ref[1:2, :] == row).astype(F32)
    full[2] = (
        counts * rate
        + jnp.where(row == col, 1.0 - growth - rate, 0.0)
        + jnp.where(row == col + 1, growth, 0.0)
    )


def functionals(full, rank):
    start = pl.multiple_of(rank * OWN, OWN)
    window = iota((WIN, PIV), 1) == iota((WIN, PIV), 0) + (start - (WIN - OWN))
    hi, lo = split(jnp.concatenate([full[m, pl.ds(start, OWN), :] for m in range(3)], axis=0))
    top = jnp.concatenate([window.astype(BF16), hi], axis=0)
    return jnp.concatenate(
        [
            jnp.concatenate([top, top], axis=1),
            jnp.concatenate([lo, jnp.zeros_like(lo)], axis=1),
        ],
        axis=0,
    )


def apply(func, hi, lo):
    got = dot(func, jnp.concatenate([hi, lo], axis=0))
    return jnp.concatenate([got[0:WIN], got[WIN:ROWS] + got[ROWS:]], axis=0)


def place():
    rank, cell = lax.axis_index("pairs"), lax.axis_index("cells")
    part, odd = lax.rem(cell, 4), lax.rem(cell, 2)
    partner = rank + jnp.where((part == 0) | (part == 3), 1 - 2 * lax.rem(rank, 2), 0)
    return rank, partner, odd


def pick_two(sent):
    named = jnp.concatenate([sent, sent + COLS], axis=1)
    return (iota((2 * COLS, 2 * SLOTS), 0) == named).astype(BF16)


def start_loads(number, held, sem, cuts):
    loads = [
        pltpu.make_async_copy(
            number.at[pl.ds(a, b - a)], held.at[pl.ds(a - cuts[0], b - a)], sem.at[i]
        )
        for i, (a, b) in enumerate(zip(cuts, cuts[1:]))
    ]
    loads[0].start()
    return loads


def copy_all(sources, targets, sem):
    copies = [
        pltpu.make_async_copy(a, b, sem.at[i]) for i, (a, b) in enumerate(zip(sources, targets))
    ]
    for copy in copies:
        copy.start()
    return copies


def halo_kernel(number, *refs, cuts):
    source, (out, held), small = refs[:6], refs[6:8], refs[8:14]
    full, pick, func, load_sem, small_sem = refs[14:]
    sends, kernel, growth, rate, target, table = small
    loads = start_loads(number, held, load_sem, cuts)
    copies = copy_all((*source[:5], source[5].at[0:2]), small, small_sem)
    for copy in loads[1:AHEAD]:
        copy.start()
    for copy in copies:
        copy.wait()

    _, partner, odd = place()
    fill_functionals(full, kernel, growth, rate, target, table)
    func[...] = functionals(full, partner)
    pick[...] = pick_two(jnp.where(odd == 1, sends[0:1, :], sends[1:2, :]))

    for i, (start, stop) in enumerate(zip(cuts, cuts[1:])):
        loads[i].wait()
        if i + AHEAD < len(loads):
            loads[i + AHEAD].start()
        for s in range(start - cuts[0], stop - cuts[0], STEP):
            both = jnp.concatenate(
                [
                    jnp.concatenate([held[s + 2 * q], held[s + 2 * q + 1]], axis=1)
                    for q in range(STEP // 2)
                ],
                axis=0,
            )
            hi, lo = split(both)
            got_hi = dot(hi, pick[...]).astype(BF16)
            got_lo = dot(lo, pick[...]).astype(BF16)
            for q in range(0, STEP // 2, 2):
                a, b = slice(q * PIV, (q + 1) * PIV), slice((q + 1) * PIV, (q + 2) * PIV)
                got = apply(
                    func[...],
                    jnp.concatenate([got_hi[a], got_hi[b]], axis=1),
                    jnp.concatenate([got_lo[a], got_lo[b]], axis=1),
                )
                out[s // 2 + q] = got[:, 0 : 2 * SLOTS]
                out[s // 2 + q + 1] = got[:, 2 * SLOTS :]


def local_kernel(number, *refs, cuts):
    source, (base, *near), refs = refs[:8], refs[8 : 9 + NEAR], refs[9 + NEAR :]
    came, band, held, small = *refs[:3], refs[3:11]
    full, mixing, func, pick, load_sem, small_sem = refs[11:]
    sends, mix, neighbours, kernel, growth, rate, target, table = small
    loads = start_loads(number, held, load_sem, cuts)
    copies = copy_all(source, small, small_sem)
    for copy in loads[1:AHEAD]:
        copy.start()
    for copy in copies:
        copy.wait()

    rank, _, odd = place()
    fill_functionals(full, kernel, growth, rate, target, table)
    func[...] = functionals(full, rank)
    pick[...] = pick_two(jnp.where(odd == 1, sends[1:2, :], sends[0:1, :]))
    row, col = iota((COLS, COLS), 0), iota((COLS, COLS), 1)
    m = mix[...]
    total = jnp.where(row == col, 1.0 - m[0:1] - m[1:2] - m[2:3], 0.0)
    for e in range(3):
        total = total + jnp.where(neighbours[e : e + 1, :] == row, m[e : e + 1], 0.0)
    mixing[0], mixing[1] = split(total)

    row = iota((4 * SLOTS, COLS), 0)
    inner = lax.rem(row, 2 * SLOTS)
    upper = jnp.where(row < 2 * SLOTS, 1 - odd, odd)
    for a in range(2):
        slot = COLS + upper * SLOTS + inner - a * SLOTS
        slot = jnp.where((inner >= a * SLOTS) & (inner < (a + 1) * SLOTS), slot, -1)
        total = jnp.zeros((4 * SLOTS, COLS), F32)
        for e in range(3):
            total = total + jnp.where(neighbours[e : e + 1, :] == slot, m[e : e + 1], 0.0)
        hi, lo = split(total)
        came[0, :, a * COLS : (a + 1) * COLS] = hi
        came[1, :, a * COLS : (a + 1) * COLS] = lo
    sym = symmetric(kernel)
    start = pl.multiple_of(rank * OWN, OWN)
    shift = lax.rem(PIV + (WIN - OWN) - rank * OWN, PIV)
    rows = []
    for m in range(2, 5):
        full[m - 2] = pltpu.roll(sym, m, 0) * table[m]
        rows.append(full[m - 2, pl.ds(start, OWN), :])
    hi, lo = split(pltpu.roll(jnp.concatenate(rows, axis=0), shift, 1)[:, 0:WIN])
    band[...] = jnp.concatenate([hi, hi, lo], axis=1)

    pairs = STEP // 2
    for i, (start, stop) in enumerate(zip(cuts, cuts[1:])):
        loads[i].wait()
        if i + AHEAD < len(loads):
            loads[i + AHEAD].start()
        for s in range(start, stop, STEP):
            parts = [apply(func[...], *split(held[l])) for l in range(s, s + STEP)]
            t_hi, t_lo = split(jnp.concatenate(parts, axis=0))
            mixed = dot(t_hi, mixing[0]) + dot(t_lo, mixing[0]) + dot(t_hi, mixing[1])
            base[s : s + STEP] = mixed.reshape(STEP, ROWS, COLS)

            def two(t):
                rows = [t[l * ROWS : (l + 1) * ROWS] for l in range(STEP)]
                return jnp.concatenate(
                    [jnp.concatenate(rows[2 * q : 2 * q + 2], axis=1) for q in range(pairs)], axis=0
                )

            got = dot(two(t_hi), pick[...]) + dot(two(t_lo), pick[...])
            piece = near[0].shape[0]
            at = s // 2 % piece
            near[s // 2 // piece][at : at + pairs] = got.reshape(pairs, ROWS, 2 * SLOTS)


def update_kernel(base, came, band, far, *rest, first):
    near = rest[:NEAR]
    piece = near[0].shape[0]
    out, done, store_sem = rest[-3:]
    pairs = STEP // 2
    own = WIN - OWN
    stores = []
    for i, s in enumerate(range(0, done.shape[0], STEP)):
        both = jnp.concatenate(
            [
                jnp.concatenate(
                    [near[(first + s) // 2 // piece][(first + s) // 2 % piece + q], far[s // 2 + q]],
                    axis=1,
                )
                for q in range(pairs)
            ],
            axis=0,
        )
        hi, lo = split(both)
        got = dot(hi, came[0]) + dot(lo, came[0]) + dot(hi, came[1])
        for l in range(STEP):
            q, a = l // 2, l % 2
            v = base[first + s + l] + got[q * ROWS : (q + 1) * ROWS, a * COLS : (a + 1) * COLS]
            window = v[0:WIN]
            n_hi, n_lo = split(window)
            births = dot(band[...], jnp.concatenate([n_hi, n_lo, n_hi], axis=0))
            total = v[WIN + 2 * OWN : WIN + 3 * OWN] + window[own:] * v[WIN : WIN + OWN]
            total = total + window[own - 1 : WIN - 1] * v[WIN + OWN : WIN + 2 * OWN]
            for m in range(2, 5):
                total = total + window[own - m : WIN - m] * births[(m - 2) * OWN : (m - 1) * OWN]
            done[s + l] = total
        stores.append(
            pltpu.make_async_copy(
                done.at[pl.ds(s, STEP)], out.at[pl.ds(first + s, STEP)], store_sem.at[i]
            )
        )
        stores[-1].start()
    for copy in stores:
        copy.wait()


def on_device(number, mix, neighbours, sends, kernel, growth, brk_rate, brk_target):
    levels = number.shape[0]
    growth = growth.reshape(1, PIV)
    rate = brk_rate.reshape(1, PIV)
    table = jnp.asarray(share_tables())
    hbm = pl.BlockSpec(memory_space=pltpu.HBM)
    vmem = pl.BlockSpec(memory_space=pltpu.VMEM)
    shape = jax.ShapeDtypeStruct
    cost = pl.CostEstimate(flops=10**6, bytes_accessed=10**6, transcendentals=0)

    def params(mib):
        return pltpu.CompilerParams(vmem_limit_bytes=mib * 2**20)

    n_cells, n_pairs = lax.axis_size("cells"), lax.axis_size("pairs")
    far_pairs, near_pairs = [], []
    for d in range(n_cells):
        for p in range(n_pairs):
            near_pairs.append((d * n_pairs + p, (d ^ 1) * n_pairs + p))
            to = d + 1 if d % 2 else d - 1
            if 0 <= to < n_cells:
                far_pairs.append((d * n_pairs + p, to * n_pairs + (p ^ (d % 4 in (0, 3)))))

    small = (sends, mix, neighbours, kernel, growth, rate, brk_target, table)
    halo_small = (sends, kernel, growth, rate, brk_target, table)

    def scratch(arrays):
        return [pltpu.VMEM(x.shape, x.dtype) for x in arrays]

    far = []
    for first, last in zip((0,) + SPLITS, SPLITS + (levels,)):
        cuts = tuple(range(first, last + 1, LOAD))
        message = pl.pallas_call(
            functools.partial(halo_kernel, cuts=cuts),
            in_specs=[hbm] * 7,
            out_specs=vmem,
            out_shape=shape(((last - first) // 2, ROWS, 2 * SLOTS), F32),
            scratch_shapes=[pltpu.VMEM((last - first, PIV, COLS), F32)]
            + scratch(halo_small[:5] + (table[0:2],))
            + [
                pltpu.VMEM((3, PIV, PIV), F32),
                pltpu.VMEM((2 * COLS, 2 * SLOTS), BF16),
                pltpu.VMEM((ROWS + 3 * OWN, 2 * PIV), BF16),
                pltpu.SemaphoreType.DMA((len(cuts) - 1,)),
                pltpu.SemaphoreType.DMA((6,)),
            ],
            compiler_params=params(LIMITS[0]),
            cost_estimate=cost,
            name=f"halo{first}",
        )(number, *halo_small)
        far.append((first, lax.ppermute(message, ("cells", "pairs"), far_pairs)))

    cuts = tuple(range(0, levels + 1, LOAD))
    base, *near, came, band = pl.pallas_call(
        functools.partial(local_kernel, cuts=cuts),
        in_specs=[hbm] * 9,
        out_specs=[vmem] * (3 + NEAR),
        out_shape=[shape((levels, ROWS, COLS), F32)]
        + [shape((levels // 2 // NEAR, ROWS, 2 * SLOTS), F32)] * NEAR
        + [shape((2, 4 * SLOTS, 2 * COLS), BF16), shape((3 * OWN, 3 * WIN), BF16)],
        scratch_shapes=[pltpu.VMEM(number.shape, F32)]
        + scratch(small)
        + [
            pltpu.VMEM((3, PIV, PIV), F32),
            pltpu.VMEM((2, COLS, COLS), BF16),
            pltpu.VMEM((ROWS + 3 * OWN, 2 * PIV), BF16),
            pltpu.VMEM((2 * COLS, 2 * SLOTS), BF16),
            pltpu.SemaphoreType.DMA((len(cuts) - 1,)),
            pltpu.SemaphoreType.DMA((len(small),)),
        ],
        compiler_params=params(LIMITS[1]),
        cost_estimate=cost,
        name="local",
    )(number, *small)
    near = [lax.ppermute(x, ("cells", "pairs"), near_pairs) for x in near]

    out = ()
    for first, message in far:
        count = 2 * message.shape[0]
        out = (
            pl.pallas_call(
                functools.partial(update_kernel, first=first),
                in_specs=[vmem] * (4 + NEAR) + [hbm] * len(out),
                out_specs=hbm,
                out_shape=shape((levels, OWN, COLS), F32),
                input_output_aliases={4 + NEAR: 0} if out else {},
                scratch_shapes=[
                    pltpu.VMEM((count, OWN, COLS), F32),
                    pltpu.SemaphoreType.DMA((count // STEP,)),
                ],
                compiler_params=params(LIMITS[2]),
                cost_estimate=cost,
                name=f"update{first}",
            )(base, came, band, message, *near, *out),
        )
    return out[0]


def solution(mesh):
    placed = (
        P(None, None, "cells"),
        P(None, "cells"),
        P(None, "cells"),
        P(None, "cells"),
        P(),
        P(),
        P(),
        P(),
    )
    return jax.shard_map(
        on_device, mesh=mesh, in_specs=placed, out_specs=P(None, "pairs", "cells"), check_vma=False
    )
```

```python
import functools

import jax
import jax.numpy as jnp
import numpy as np
from jax import lax
from jax.experimental import pallas as pl
from jax.experimental.pallas import tpu as pltpu
from jax.sharding import PartitionSpec as P

PIV = 128
COLS = 256
SLOTS = 64
OWN = 16
WIN = 32
ROWS = WIN + 3 * OWN
STEP = 16
SPLITS = ()
NEAR = 2
HALO_CUTS = (0, 16, 32, 48, 64)
LOAD = 16
AHEAD = 3
LIMITS = (54, 46, 32)
F32 = jnp.float32
BF16 = jnp.bfloat16


def share_tables():
    v = 2.0 ** (np.arange(PIV) / 4.0)
    tables = np.zeros((5, PIV, PIV))
    for m in range(5):
        for k in range(m, PIV):
            i = k - m
            for j in range(i + 1):
                u = 2.0 ** ((i + 4) / 4.0) if i == j else v[i] + v[j]
                if i == j and i + 4 < PIV:
                    u = v[i + 4]
                share = 0.0
                if k >= 1 and v[k - 1] < u <= v[k]:
                    share = (u - v[k - 1]) / (v[k] - v[k - 1])
                elif k <= PIV - 2 and v[k] < u < v[k + 1]:
                    share = (v[k + 1] - u) / (v[k + 1] - v[k])
                elif k == PIV - 1 and u > v[k]:
                    share = u / v[k]
                tables[m, k, j] = share * (0.5 if i == j else 1.0)
    return tables.astype(np.float32)


def split(x):
    hi = x.astype(BF16)
    return hi, (x - hi.astype(F32)).astype(BF16)


def dot(a, b):
    return jnp.dot(a, b, preferred_element_type=F32)


def iota(shape, axis):
    return lax.broadcasted_iota(jnp.int32, shape, axis)


def symmetric(kernel_ref):
    k = kernel_ref[...]
    return 0.5 * (k + k.T)


def fill_functionals(full, kernel_ref, growth_ref, rate_ref, target_ref, table_ref):
    sym = symmetric(kernel_ref)
    full[0] = sym * (table_ref[0] - 1.0)
    full[1] = pltpu.roll(sym, 1, 0) * table_ref[1]
    row, col = iota((PIV, PIV), 0), iota((PIV, PIV), 1)
    rate, growth = rate_ref[...], growth_ref[...]
    counts = (target_ref[0:1, :] == row).astype(F32) + (target_ref[1:2, :] == row).astype(F32)
    full[2] = (
        counts * rate
        + jnp.where(row == col, 1.0 - growth - rate, 0.0)
        + jnp.where(row == col + 1, growth, 0.0)
    )


def functionals(full, rank):
    start = pl.multiple_of(rank * OWN, OWN)
    window = iota((WIN, PIV), 1) == iota((WIN, PIV), 0) + (start - (WIN - OWN))
    hi, lo = split(jnp.concatenate([full[m, pl.ds(start, OWN), :] for m in range(3)], axis=0))
    top = jnp.concatenate([window.astype(BF16), hi], axis=0)
    return jnp.concatenate(
        [
            jnp.concatenate([top, top], axis=1),
            jnp.concatenate([lo, jnp.zeros_like(lo)], axis=1),
        ],
        axis=0,
    )


def apply(func, hi, lo):
    got = dot(func, jnp.concatenate([hi, lo], axis=0))
    return jnp.concatenate([got[0:WIN], got[WIN:ROWS] + got[ROWS:]], axis=0)


def place():
    rank, cell = lax.axis_index("pairs"), lax.axis_index("cells")
    part, odd = lax.rem(cell, 4), lax.rem(cell, 2)
    partner = rank + jnp.where((part == 0) | (part == 3), 1 - 2 * lax.rem(rank, 2), 0)
    return rank, partner, odd


def pick_two(sent):
    named = jnp.concatenate([sent, sent + COLS], axis=1)
    return (iota((2 * COLS, 2 * SLOTS), 0) == named).astype(BF16)


def start_loads(number, held, sem, cuts):
    loads = [
        pltpu.make_async_copy(
            number.at[pl.ds(a, b - a)], held.at[pl.ds(a - cuts[0], b - a)], sem.at[i]
        )
        for i, (a, b) in enumerate(zip(cuts, cuts[1:]))
    ]
    loads[0].start()
    return loads


def copy_all(sources, targets, sem):
    copies = [
        pltpu.make_async_copy(a, b, sem.at[i]) for i, (a, b) in enumerate(zip(sources, targets))
    ]
    for copy in copies:
        copy.start()
    return copies


def halo_kernel(number, *refs, cuts):
    source, (out, held), small = refs[:6], refs[6:8], refs[8:14]
    full, pick, func, made, load_sem, small_sem, store_sem = refs[14:]
    sends, kernel, growth, rate, target, table = small
    stores = []
    copies = copy_all((*source[:5], source[5].at[0:2]), small, small_sem)
    loads = start_loads(number, held, load_sem, cuts)
    for copy in copies:
        copy.wait()
    for copy in loads[1:AHEAD]:
        copy.start()

    _, partner, odd = place()
    fill_functionals(full, kernel, growth, rate, target, table)
    func[...] = functionals(full, partner)
    sent = jnp.where(odd == 1, sends[0:1, :], sends[1:2, :])
    named = jnp.broadcast_to(jnp.concatenate([sent, sent], axis=1), (PIV, 2 * SLOTS))
    lane, upper = lax.rem(named, PIV), named >= PIV
    even = iota((PIV, 2 * SLOTS), 1) < SLOTS

    for i, (start, stop) in enumerate(zip(cuts, cuts[1:])):
        loads[i].wait()
        if i + AHEAD < len(loads):
            loads[i + AHEAD].start()
        s, pairs = start - cuts[0], (stop - start) // 2
        def taken(l):
            x = held[s + l]
            a = jnp.take_along_axis(x[:, :PIV], lane, axis=1)
            b = jnp.take_along_axis(x[:, PIV:], lane, axis=1)
            return jnp.where(upper, b, a)

        got_hi, got_lo = split(
            jnp.concatenate(
                [jnp.where(even, taken(2 * q), taken(2 * q + 1)) for q in range(pairs)], axis=0
            )
        )
        for q in range(0, pairs, 2):
            a, b = slice(q * PIV, (q + 1) * PIV), slice((q + 1) * PIV, (q + 2) * PIV)
            got = apply(
                func[...],
                jnp.concatenate([got_hi[a], got_hi[b]], axis=1),
                jnp.concatenate([got_lo[a], got_lo[b]], axis=1),
            )
            made[s // 2 + q] = got[:, 0 : 2 * SLOTS]
            made[s // 2 + q + 1] = got[:, 2 * SLOTS :]
        rows = pl.ds(s // 2, pairs)
        stores.append(pltpu.make_async_copy(made.at[rows], out.at[rows], store_sem.at[i]))
        stores[-1].start()
    for copy in stores:
        copy.wait()


def local_kernel(number, *refs, cuts):
    source, (base, *near), refs = refs[:8], refs[8 : 9 + NEAR], refs[9 + NEAR :]
    came, band, held, small = *refs[:3], refs[3:11]
    full, mixing, func, pick, load_sem, small_sem = refs[11:]
    sends, mix, neighbours, kernel, growth, rate, target, table = small
    loads = start_loads(number, held, load_sem, cuts)
    copies = copy_all(source, small, small_sem)
    for copy in loads[1:AHEAD]:
        copy.start()
    for copy in copies:
        copy.wait()

    rank, _, odd = place()
    fill_functionals(full, kernel, growth, rate, target, table)
    func[...] = functionals(full, rank)
    pick[...] = pick_two(jnp.where(odd == 1, sends[1:2, :], sends[0:1, :]))
    row, col = iota((COLS, COLS), 0), iota((COLS, COLS), 1)
    m = mix[...]
    total = jnp.where(row == col, 1.0 - m[0:1] - m[1:2] - m[2:3], 0.0)
    for e in range(3):
        total = total + jnp.where(neighbours[e : e + 1, :] == row, m[e : e + 1], 0.0)
    mixing[0], mixing[1] = split(total)

    row = iota((2 * SLOTS, COLS), 0)
    for way in range(2):
        upper = 1 - odd if way == 0 else odd
        for a in range(2):
            slot = COLS + upper * SLOTS + row - a * SLOTS
            slot = jnp.where((row >= a * SLOTS) & (row < (a + 1) * SLOTS), slot, -1)
            total = jnp.zeros((2 * SLOTS, COLS), F32)
            for e in range(3):
                total = total + jnp.where(neighbours[e : e + 1, :] == slot, m[e : e + 1], 0.0)
            hi, lo = split(total)
            lanes = slice(a * COLS, (a + 1) * COLS)
            came[way, 0 : 2 * SLOTS, lanes] = hi
            came[way, 2 * SLOTS : 4 * SLOTS, lanes] = hi
            came[way, 4 * SLOTS :, lanes] = lo
    sym = symmetric(kernel)
    start = pl.multiple_of(rank * OWN, OWN)
    shift = lax.rem(PIV + (WIN - OWN) - rank * OWN, PIV)
    rows = []
    for m in range(2, 5):
        full[m - 2] = pltpu.roll(sym, m, 0) * table[m]
        rows.append(full[m - 2, pl.ds(start, OWN), :])
    hi, lo = split(pltpu.roll(jnp.concatenate(rows, axis=0), shift, 1)[:, 0:WIN])
    band[...] = jnp.concatenate([hi, hi, lo], axis=1)

    pairs = STEP // 2
    for i, (start, stop) in enumerate(zip(cuts, cuts[1:])):
        loads[i].wait()
        if i + AHEAD < len(loads):
            loads[i + AHEAD].start()
        for s in range(start, stop, STEP):
            parts = [apply(func[...], *split(held[l])) for l in range(s, s + STEP)]
            t_hi, t_lo = split(jnp.concatenate(parts, axis=0))
            mixed = dot(t_hi, mixing[0]) + dot(t_lo, mixing[0]) + dot(t_hi, mixing[1])
            base[s : s + STEP] = mixed.reshape(STEP, ROWS, COLS)

            def two(t):
                rows = [t[l * ROWS : (l + 1) * ROWS] for l in range(STEP)]
                return jnp.concatenate(
                    [jnp.concatenate(rows[2 * q : 2 * q + 2], axis=1) for q in range(pairs)], axis=0
                )

            got = dot(two(t_hi), pick[...]) + dot(two(t_lo), pick[...])
            piece = near[0].shape[0]
            at = s // 2 % piece
            near[s // 2 // piece][at : at + pairs] = got.reshape(pairs, ROWS, 2 * SLOTS)


def spread(message, came):
    hi, lo = split(message)
    return dot(jnp.concatenate([hi, lo], axis=1), came[0 : 4 * SLOTS]) + dot(hi, came[4 * SLOTS :])


def near_kernel(base, came, *refs):
    *near, out = refs
    count = STEP // 2 * ROWS
    piece = near[0].shape[0]
    for s in range(0, base.shape[0], STEP):
        at = s // 2 % piece
        part = near[s // 2 // piece][at : at + STEP // 2]
        got = spread(part.reshape(count, 2 * SLOTS), came[0])
        for l in range(STEP):
            q, a = l // 2, l % 2
            out[s + l] = base[s + l] + got[q * ROWS : (q + 1) * ROWS, a * COLS : (a + 1) * COLS]


def update_kernel(base, came, band, far, out, done, store_sem):
    own = WIN - OWN
    count = STEP // 2 * ROWS
    stores = []
    for i, s in enumerate(range(0, base.shape[0], STEP)):
        got = spread(far[s // 2 : (s + STEP) // 2].reshape(count, 2 * SLOTS), came[1])
        for l in range(STEP):
            q, a = l // 2, l % 2
            v = base[s + l] + got[q * ROWS : (q + 1) * ROWS, a * COLS : (a + 1) * COLS]
            window = v[0:WIN]
            n_hi, n_lo = split(window)
            births = dot(band[...], jnp.concatenate([n_hi, n_lo, n_hi], axis=0))
            total = v[WIN + 2 * OWN : WIN + 3 * OWN] + window[own:] * v[WIN : WIN + OWN]
            total = total + window[own - 1 : WIN - 1] * v[WIN + OWN : WIN + 2 * OWN]
            for m in range(2, 5):
                total = total + window[own - m : WIN - m] * births[(m - 2) * OWN : (m - 1) * OWN]
            done[s + l] = total
        rows = pl.ds(s, STEP)
        stores.append(pltpu.make_async_copy(done.at[rows], out.at[rows], store_sem.at[i]))
        stores[-1].start()
    for copy in stores:
        copy.wait()


def on_device(number, mix, neighbours, sends, kernel, growth, brk_rate, brk_target):
    levels = number.shape[0]
    growth = growth.reshape(1, PIV)
    rate = brk_rate.reshape(1, PIV)
    table = jnp.asarray(share_tables())
    hbm = pl.BlockSpec(memory_space=pltpu.HBM)
    vmem = pl.BlockSpec(memory_space=pltpu.VMEM)
    shape = jax.ShapeDtypeStruct
    cost = pl.CostEstimate(flops=10**6, bytes_accessed=10**6, transcendentals=0)

    def params(mib):
        return pltpu.CompilerParams(vmem_limit_bytes=mib * 2**20)

    n_cells, n_pairs = lax.axis_size("cells"), lax.axis_size("pairs")
    far_pairs, near_pairs = [], []
    for d in range(n_cells):
        for p in range(n_pairs):
            near_pairs.append((d * n_pairs + p, (d ^ 1) * n_pairs + p))
            to = d + 1 if d % 2 else d - 1
            if 0 <= to < n_cells:
                far_pairs.append((d * n_pairs + p, to * n_pairs + (p ^ (d % 4 in (0, 3)))))

    small = (sends, mix, neighbours, kernel, growth, rate, brk_target, table)
    halo_small = (sends, kernel, growth, rate, brk_target, table)

    def scratch(arrays):
        return [pltpu.VMEM(x.shape, x.dtype) for x in arrays]

    far = []
    for first, last in zip((0,) + SPLITS, SPLITS + (levels,)):
        cuts = HALO_CUTS
        message = pl.pallas_call(
            functools.partial(halo_kernel, cuts=cuts),
            in_specs=[hbm] * 7,
            out_specs=hbm,
            out_shape=shape(((last - first) // 2, ROWS, 2 * SLOTS), F32),
            scratch_shapes=[pltpu.VMEM((last - first, PIV, COLS), F32)]
            + scratch(halo_small[:5] + (table[0:2],))
            + [
                pltpu.VMEM((3, PIV, PIV), F32),
                pltpu.VMEM((2 * COLS, 2 * SLOTS), BF16),
                pltpu.VMEM((ROWS + 3 * OWN, 2 * PIV), BF16),
                pltpu.VMEM(((last - first) // 2, ROWS, 2 * SLOTS), F32),
                pltpu.SemaphoreType.DMA((len(cuts) - 1,)),
                pltpu.SemaphoreType.DMA((6,)),
                pltpu.SemaphoreType.DMA((len(cuts) - 1,)),
            ],
            compiler_params=params(LIMITS[0]),
            cost_estimate=cost,
            name=f"halo{first}",
        )(number, *halo_small)
        far.append((first, lax.ppermute(message, ("cells", "pairs"), far_pairs)))

    cuts = tuple(range(0, levels + 1, LOAD))
    base, *near, came, band = pl.pallas_call(
        functools.partial(local_kernel, cuts=cuts),
        in_specs=[hbm] * 9,
        out_specs=[vmem] * (3 + NEAR),
        out_shape=[shape((levels, ROWS, COLS), F32)]
        + [shape((levels // 2 // NEAR, ROWS, 2 * SLOTS), F32)] * NEAR
        + [shape((2, 6 * SLOTS, 2 * COLS), BF16), shape((3 * OWN, 3 * WIN), BF16)],
        scratch_shapes=[pltpu.VMEM(number.shape, F32)]
        + scratch(small)
        + [
            pltpu.VMEM((3, PIV, PIV), F32),
            pltpu.VMEM((2, COLS, COLS), BF16),
            pltpu.VMEM((ROWS + 3 * OWN, 2 * PIV), BF16),
            pltpu.VMEM((2 * COLS, 2 * SLOTS), BF16),
            pltpu.SemaphoreType.DMA((len(cuts) - 1,)),
            pltpu.SemaphoreType.DMA((len(small),)),
        ],
        compiler_params=params(LIMITS[1]),
        cost_estimate=cost,
        name="local",
    )(number, *small)
    near = [lax.ppermute(x, ("cells", "pairs"), near_pairs) for x in near]

    base = pl.pallas_call(
        near_kernel,
        in_specs=[vmem] * (2 + NEAR),
        out_specs=vmem,
        out_shape=shape(base.shape, F32),
        input_output_aliases={0: 0},
        compiler_params=params(LIMITS[2]),
        cost_estimate=cost,
        name="near",
    )(base, came, *near)
    [(_, message)] = far
    return pl.pallas_call(
        update_kernel,
        in_specs=[vmem] * 4,
        out_specs=hbm,
        out_shape=shape((levels, OWN, COLS), F32),
        scratch_shapes=[
            pltpu.VMEM((levels, OWN, COLS), F32),
            pltpu.SemaphoreType.DMA((levels // STEP,)),
        ],
        compiler_params=params(LIMITS[2]),
        cost_estimate=cost,
        name="update",
    )(base, came, band, message)


def solution(mesh):
    placed = (
        P(None, None, "cells"),
        P(None, "cells"),
        P(None, "cells"),
        P(None, "cells"),
        P(),
        P(),
        P(),
        P(),
    )
    return jax.shard_map(
        on_device, mesh=mesh, in_specs=placed, out_specs=P(None, "pairs", "cells"), check_vma=False
    )
```

```python
import functools

import jax
import jax.numpy as jnp
import numpy as np
from jax import lax
from jax.experimental import pallas as pl
from jax.experimental.pallas import tpu as pltpu
from jax.sharding import PartitionSpec as P

PIV = 128
COLS = 256
SLOTS = 64
OWN = 16
WIN = 32
ROWS = WIN + 3 * OWN
STEP = 16
SPLITS = ()
NEAR = 2
HALO_CUTS = (0, 16, 32, 48, 64)
LOAD = 16
AHEAD = 3
LIMITS = (54, 46, 32)
F32 = jnp.float32
BF16 = jnp.bfloat16


def share_tables():
    v = 2.0 ** (np.arange(PIV) / 4.0)
    tables = np.zeros((5, PIV, PIV))
    for m in range(5):
        for k in range(m, PIV):
            i = k - m
            for j in range(i + 1):
                u = 2.0 ** ((i + 4) / 4.0) if i == j else v[i] + v[j]
                if i == j and i + 4 < PIV:
                    u = v[i + 4]
                share = 0.0
                if k >= 1 and v[k - 1] < u <= v[k]:
                    share = (u - v[k - 1]) / (v[k] - v[k - 1])
                elif k <= PIV - 2 and v[k] < u < v[k + 1]:
                    share = (v[k + 1] - u) / (v[k + 1] - v[k])
                elif k == PIV - 1 and u > v[k]:
                    share = u / v[k]
                tables[m, k, j] = share * (0.5 if i == j else 1.0)
    return tables.astype(np.float32)


def split(x):
    hi = x.astype(BF16)
    return hi, (x - hi.astype(F32)).astype(BF16)


def dot(a, b):
    return jnp.dot(a, b, preferred_element_type=F32)


def iota(shape, axis):
    return lax.broadcasted_iota(jnp.int32, shape, axis)


def symmetric(kernel_ref):
    k = kernel_ref[...]
    return 0.5 * (k + k.T)


def fill_functionals(full, kernel_ref, growth_ref, rate_ref, target_ref, table_ref):
    sym = symmetric(kernel_ref)
    full[0] = sym * (table_ref[0] - 1.0)
    full[1] = pltpu.roll(sym, 1, 0) * table_ref[1]
    row, col = iota((PIV, PIV), 0), iota((PIV, PIV), 1)
    rate, growth = rate_ref[...], growth_ref[...]
    counts = (target_ref[0:1, :] == row).astype(F32) + (target_ref[1:2, :] == row).astype(F32)
    full[2] = (
        counts * rate
        + jnp.where(row == col, 1.0 - growth - rate, 0.0)
        + jnp.where(row == col + 1, growth, 0.0)
    )


def functionals(full, rank):
    start = pl.multiple_of(rank * OWN, OWN)
    window = iota((WIN, PIV), 1) == iota((WIN, PIV), 0) + (start - (WIN - OWN))
    hi, lo = split(jnp.concatenate([full[m, pl.ds(start, OWN), :] for m in range(3)], axis=0))
    top = jnp.concatenate([window.astype(BF16), hi], axis=0)
    return jnp.concatenate(
        [
            jnp.concatenate([top, top], axis=1),
            jnp.concatenate([lo, jnp.zeros_like(lo)], axis=1),
        ],
        axis=0,
    )


def apply(func, hi, lo):
    got = dot(func, jnp.concatenate([hi, lo], axis=0))
    return jnp.concatenate([got[0:WIN], got[WIN:ROWS] + got[ROWS:]], axis=0)


def place():
    rank, cell = lax.axis_index("pairs"), lax.axis_index("cells")
    part, odd = lax.rem(cell, 4), lax.rem(cell, 2)
    partner = rank + jnp.where((part == 0) | (part == 3), 1 - 2 * lax.rem(rank, 2), 0)
    return rank, partner, odd


def pick_two(sent):
    named = jnp.concatenate([sent, sent + COLS], axis=1)
    return (iota((2 * COLS, 2 * SLOTS), 0) == named).astype(BF16)


def start_loads(number, held, sem, cuts):
    loads = [
        pltpu.make_async_copy(
            number.at[pl.ds(a, b - a)], held.at[pl.ds(a - cuts[0], b - a)], sem.at[i]
        )
        for i, (a, b) in enumerate(zip(cuts, cuts[1:]))
    ]
    loads[0].start()
    return loads


def copy_all(sources, targets, sem):
    copies = [
        pltpu.make_async_copy(a, b, sem.at[i]) for i, (a, b) in enumerate(zip(sources, targets))
    ]
    for copy in copies:
        copy.start()
    return copies


def halo_kernel(number, *refs, cuts):
    source, (out, held), small = refs[:6], refs[6:8], refs[8:14]
    full, pick, func, made, load_sem, small_sem, store_sem = refs[14:]
    sends, kernel, growth, rate, target, table = small
    stores = []
    copies = copy_all((*source[:5], source[5].at[0:2]), small, small_sem)
    loads = start_loads(number, held, load_sem, cuts)
    for copy in copies:
        copy.wait()
    for copy in loads[1:AHEAD]:
        copy.start()

    _, partner, odd = place()
    fill_functionals(full, kernel, growth, rate, target, table)
    func[...] = functionals(full, partner)
    sent = jnp.where(odd == 1, sends[0:1, :], sends[1:2, :])
    named = jnp.broadcast_to(jnp.concatenate([sent, sent], axis=1), (PIV, 2 * SLOTS))
    lane, upper = lax.rem(named, PIV), named >= PIV
    even = iota((PIV, 2 * SLOTS), 1) < SLOTS

    for i, (start, stop) in enumerate(zip(cuts, cuts[1:])):
        loads[i].wait()
        if i + AHEAD < len(loads):
            loads[i + AHEAD].start()
        s, pairs = start - cuts[0], (stop - start) // 2
        def taken(l):
            x = held[s + l]
            a = jnp.take_along_axis(x[:, :PIV], lane, axis=1)
            b = jnp.take_along_axis(x[:, PIV:], lane, axis=1)
            return jnp.where(upper, b, a)

        got_hi, got_lo = split(
            jnp.concatenate(
                [jnp.where(even, taken(2 * q), taken(2 * q + 1)) for q in range(pairs)], axis=0
            )
        )
        for q in range(0, pairs, 2):
            a, b = slice(q * PIV, (q + 1) * PIV), slice((q + 1) * PIV, (q + 2) * PIV)
            got = apply(
                func[...],
                jnp.concatenate([got_hi[a], got_hi[b]], axis=1),
                jnp.concatenate([got_lo[a], got_lo[b]], axis=1),
            )
            made[s // 4 + q // 2] = pack(got[:, 0 : 2 * SLOTS], got[:, 2 * SLOTS :])
        rows = pl.ds(s // 4, pairs // 2)
        stores.append(pltpu.make_async_copy(made.at[rows], out.at[rows], store_sem.at[i]))
        stores[-1].start()
    for copy in stores:
        copy.wait()


def local_kernel(number, *refs, cuts):
    source, (base, *near), refs = refs[:8], refs[8 : 9 + NEAR], refs[9 + NEAR :]
    came, band, held, small = *refs[:3], refs[3:11]
    full, mixing, func, pick, load_sem, small_sem = refs[11:]
    sends, mix, neighbours, kernel, growth, rate, target, table = small
    loads = start_loads(number, held, load_sem, cuts)
    copies = copy_all(source, small, small_sem)
    for copy in loads[1:AHEAD]:
        copy.start()
    for copy in copies:
        copy.wait()

    rank, _, odd = place()
    fill_functionals(full, kernel, growth, rate, target, table)
    func[...] = functionals(full, rank)
    pick[...] = pick_two(jnp.where(odd == 1, sends[1:2, :], sends[0:1, :]))
    row, col = iota((COLS, COLS), 0), iota((COLS, COLS), 1)
    m = mix[...]
    total = jnp.where(row == col, 1.0 - m[0:1] - m[1:2] - m[2:3], 0.0)
    for e in range(3):
        total = total + jnp.where(neighbours[e : e + 1, :] == row, m[e : e + 1], 0.0)
    mixing[0], mixing[1] = split(total)

    row = iota((2 * SLOTS, COLS), 0)
    for way in range(2):
        upper = 1 - odd if way == 0 else odd
        slot = COLS + upper * SLOTS + lax.rem(row, SLOTS)
        total = jnp.zeros((2 * SLOTS, COLS), F32)
        for e in range(3):
            total = total + jnp.where(neighbours[e : e + 1, :] == slot, m[e : e + 1], 0.0)
        hi = total.astype(BF16)
        low = total - hi.astype(F32)
        for a in range(2):
            came[way, a, 0 : 2 * SLOTS] = hi
            there = (row >= a * SLOTS) & (row < (a + 1) * SLOTS)
            came[way, a, 2 * SLOTS :] = jnp.where(there, low, 0.0).astype(BF16)
    sym = symmetric(kernel)
    start = pl.multiple_of(rank * OWN, OWN)
    shift = lax.rem(PIV + (WIN - OWN) - rank * OWN, PIV)
    rows = []
    for m in range(2, 5):
        full[m - 2] = pltpu.roll(sym, m, 0) * table[m]
        rows.append(full[m - 2, pl.ds(start, OWN), :])
    hi, lo = split(pltpu.roll(jnp.concatenate(rows, axis=0), shift, 1)[:, 0:WIN])
    band[...] = jnp.concatenate([hi, hi, lo], axis=1)

    pairs = STEP // 2
    for i, (start, stop) in enumerate(zip(cuts, cuts[1:])):
        loads[i].wait()
        if i + AHEAD < len(loads):
            loads[i + AHEAD].start()
        for s in range(start, stop, STEP):
            parts = [apply(func[...], *split(held[l])) for l in range(s, s + STEP)]
            t_hi, t_lo = split(jnp.concatenate(parts, axis=0))
            mixed = dot(t_hi, mixing[0]) + dot(t_lo, mixing[0]) + dot(t_hi, mixing[1])
            base[s : s + STEP] = mixed.reshape(STEP, ROWS, COLS)

            def two(t):
                rows = [t[l * ROWS : (l + 1) * ROWS] for l in range(STEP)]
                return jnp.concatenate(
                    [jnp.concatenate(rows[2 * q : 2 * q + 2], axis=1) for q in range(pairs)], axis=0
                )

            got = dot(two(t_hi), pick[...]) + dot(two(t_lo), pick[...])
            piece = near[0].shape[0]
            at = s // 2 % piece
            near[s // 2 // piece][at : at + pairs] = got.reshape(pairs, ROWS, 2 * SLOTS)


def spread(message, came):
    hi = message.astype(BF16)
    high = hi.astype(F32)
    turned = pltpu.roll(message - high, SLOTS, 1)
    left = iota(message.shape, 1) < SLOTS
    first = jnp.where(left, high, turned).astype(BF16)
    second = jnp.where(left, turned, high).astype(BF16)
    return [
        dot(jnp.concatenate([part, hi], axis=1), came[a]) for a, part in enumerate((first, second))
    ]


def near_kernel(base, came, *refs):
    *near, out = refs
    count = STEP // 2 * ROWS
    piece = near[0].shape[0]
    for s in range(0, base.shape[0], STEP):
        at = s // 2 % piece
        part = near[s // 2 // piece][at : at + STEP // 2]
        got = spread(part.reshape(count, 2 * SLOTS), came[0])
        for l in range(STEP):
            q, a = l // 2, l % 2
            out[s + l] = base[s + l] + got[a][q * ROWS : (q + 1) * ROWS]


def pack(a, b):
    mixed = jnp.where(iota((8, 2 * SLOTS), 0) < 4, pltpu.roll(b[0:8], 4, 0), a[0:8])
    return jnp.concatenate([a[8:], b[8:], mixed], axis=0)


def unpack(m):
    cut = ROWS - 8
    mixed = m[2 * cut :]
    return jnp.concatenate([mixed, m[0:cut], pltpu.roll(mixed, 4, 0), m[cut : 2 * cut]], axis=0)


def update_kernel(base, came, band, far, out, done, store_sem):
    own = WIN - OWN
    stores = []
    for i, s in enumerate(range(0, base.shape[0], STEP)):
        part = [unpack(far[q]) for q in range(s // 4, (s + STEP) // 4)]
        got = spread(jnp.concatenate(part, axis=0), came[1])
        for l in range(STEP):
            q, a = l // 2, l % 2
            v = base[s + l] + got[a][q * ROWS : (q + 1) * ROWS]
            window = v[0:WIN]
            n_hi, n_lo = split(window)
            births = dot(band[...], jnp.concatenate([n_hi, n_lo, n_hi], axis=0))
            total = v[WIN + 2 * OWN : WIN + 3 * OWN] + window[own:] * v[WIN : WIN + OWN]
            total = total + window[own - 1 : WIN - 1] * v[WIN + OWN : WIN + 2 * OWN]
            for m in range(2, 5):
                total = total + window[own - m : WIN - m] * births[(m - 2) * OWN : (m - 1) * OWN]
            done[s + l] = total
        rows = pl.ds(s, STEP)
        stores.append(pltpu.make_async_copy(done.at[rows], out.at[rows], store_sem.at[i]))
        stores[-1].start()
    for copy in stores:
        copy.wait()


def on_device(number, mix, neighbours, sends, kernel, growth, brk_rate, brk_target):
    levels = number.shape[0]
    growth = growth.reshape(1, PIV)
    rate = brk_rate.reshape(1, PIV)
    table = jnp.asarray(share_tables())
    hbm = pl.BlockSpec(memory_space=pltpu.HBM)
    vmem = pl.BlockSpec(memory_space=pltpu.VMEM)
    shape = jax.ShapeDtypeStruct
    cost = pl.CostEstimate(flops=10**6, bytes_accessed=10**6, transcendentals=0)

    def params(mib):
        return pltpu.CompilerParams(vmem_limit_bytes=mib * 2**20)

    n_cells, n_pairs = lax.axis_size("cells"), lax.axis_size("pairs")
    far_pairs, near_pairs = [], []
    for d in range(n_cells):
        for p in range(n_pairs):
            near_pairs.append((d * n_pairs + p, (d ^ 1) * n_pairs + p))
            to = d + 1 if d % 2 else d - 1
            if 0 <= to < n_cells:
                far_pairs.append((d * n_pairs + p, to * n_pairs + (p ^ (d % 4 in (0, 3)))))

    small = (sends, mix, neighbours, kernel, growth, rate, brk_target, table)
    halo_small = (sends, kernel, growth, rate, brk_target, table)

    def scratch(arrays):
        return [pltpu.VMEM(x.shape, x.dtype) for x in arrays]

    far = []
    for first, last in zip((0,) + SPLITS, SPLITS + (levels,)):
        cuts = HALO_CUTS
        message = pl.pallas_call(
            functools.partial(halo_kernel, cuts=cuts),
            in_specs=[hbm] * 7,
            out_specs=hbm,
            out_shape=shape(((last - first) // 4, 2 * ROWS - 8, 2 * SLOTS), F32),
            scratch_shapes=[pltpu.VMEM((last - first, PIV, COLS), F32)]
            + scratch(halo_small[:5] + (table[0:2],))
            + [
                pltpu.VMEM((3, PIV, PIV), F32),
                pltpu.VMEM((2 * COLS, 2 * SLOTS), BF16),
                pltpu.VMEM((ROWS + 3 * OWN, 2 * PIV), BF16),
                pltpu.VMEM(((last - first) // 4, 2 * ROWS - 8, 2 * SLOTS), F32),
                pltpu.SemaphoreType.DMA((len(cuts) - 1,)),
                pltpu.SemaphoreType.DMA((6,)),
                pltpu.SemaphoreType.DMA((len(cuts) - 1,)),
            ],
            compiler_params=params(LIMITS[0]),
            cost_estimate=cost,
            name=f"halo{first}",
        )(number, *halo_small)
        far.append((first, lax.ppermute(message, ("cells", "pairs"), far_pairs)))

    cuts = tuple(range(0, levels + 1, LOAD))
    base, *near, came, band = pl.pallas_call(
        functools.partial(local_kernel, cuts=cuts),
        in_specs=[hbm] * 9,
        out_specs=[vmem] * (3 + NEAR),
        out_shape=[shape((levels, ROWS, COLS), F32)]
        + [shape((levels // 2 // NEAR, ROWS, 2 * SLOTS), F32)] * NEAR
        + [shape((2, 2, 4 * SLOTS, COLS), BF16), shape((3 * OWN, 3 * WIN), BF16)],
        scratch_shapes=[pltpu.VMEM(number.shape, F32)]
        + scratch(small)
        + [
            pltpu.VMEM((3, PIV, PIV), F32),
            pltpu.VMEM((2, COLS, COLS), BF16),
            pltpu.VMEM((ROWS + 3 * OWN, 2 * PIV), BF16),
            pltpu.VMEM((2 * COLS, 2 * SLOTS), BF16),
            pltpu.SemaphoreType.DMA((len(cuts) - 1,)),
            pltpu.SemaphoreType.DMA((len(small),)),
        ],
        compiler_params=params(LIMITS[1]),
        cost_estimate=cost,
        name="local",
    )(number, *small)
    near = [lax.ppermute(x, ("cells", "pairs"), near_pairs) for x in near]

    base = pl.pallas_call(
        near_kernel,
        in_specs=[vmem] * (2 + NEAR),
        out_specs=vmem,
        out_shape=shape(base.shape, F32),
        input_output_aliases={0: 0},
        compiler_params=params(LIMITS[2]),
        cost_estimate=cost,
        name="near",
    )(base, came, *near)
    [(_, message)] = far
    return pl.pallas_call(
        update_kernel,
        in_specs=[vmem] * 4,
        out_specs=hbm,
        out_shape=shape((levels, OWN, COLS), F32),
        scratch_shapes=[
            pltpu.VMEM((levels, OWN, COLS), F32),
            pltpu.SemaphoreType.DMA((levels // STEP,)),
        ],
        compiler_params=params(LIMITS[2]),
        cost_estimate=cost,
        name="update",
    )(base, came, band, message)


def solution(mesh):
    placed = (
        P(None, None, "cells"),
        P(None, "cells"),
        P(None, "cells"),
        P(None, "cells"),
        P(),
        P(),
        P(),
        P(),
    )
    return jax.shard_map(
        on_device, mesh=mesh, in_specs=placed, out_specs=P(None, "pairs", "cells"), check_vma=False
    )
```
